256 devices in a mesh: dp: 16 (over z, core), tensor: 16 (over y, x).
Axes of the slice: x: 4, y: 4, z: 8, core: 2. Of those that a mesh axis runs over, the one named last changes fastest.
Arguments:
- queries: bfloat16 [64, 256, 8192], P('dp', None, 'tensor'), may hold values from -5 to 5
- grad_output: bfloat16 [64, 256, 8192], P('dp', None, 'tensor'), may hold values from -5 to 5
- image_keys: bfloat16 [16, 256, 256, 128], P('tensor', 'dp'), may hold values from -5 to 5
- image_values: bfloat16 [16, 256, 256, 128], P('tensor', 'dp'), may hold values from -5 to 5
- attn_gate: float32 [1], replicated, may hold values from 0.3 to 1.2
- image_counts: int32 [64], P('dp'), may hold values from 1 to 4
- text_lengths: int32 [64], P('dp'), may hold values from 64 to 256
- tile_owner: int32 [64, 4], P('dp'), may hold values from 0 to 15, as said below
Outputs:
- grad_queries: bfloat16 [64, 256, 8192], P('dp', None, 'tensor')
- grad_keys: bfloat16 [16, 256, 256, 128], P('tensor', 'dp')
- grad_values: bfloat16 [16, 256, 256, 128], P('tensor', 'dp')
The draws below stay inside these ranges and needn't reach their ends.
Inputs may be any that keep to these rules, and one draw needn't show every extreme that they name: `tile_owner`: for each index g along dp, the 16 tiles of its samples name every index along dp exactly once.
All inputs are finite; a program needn't handle non-finite values.
Results may differ from the reference program's by a relative error of at most 0.03.
Values may be sent and summed in bfloat16 or wider, within the bound.
A program may use at most 128 MiB of HBM per device.

```python
import jax
import jax.numpy as jnp
from jax import lax

HEAD_DIM = 128
HEADS_DEV = 4
Q_GROUP = 8
HEADS = 64
KV_HEADS = 8
MAX_TILES = 4
SAMP_DEV = 4
SAMPLES = 64
TEXT = 256
TILE = 512
HALF = 256
SLOTS = 256
N_DP = 16


def draw_queries(key, part):
    key = jax.random.fold_in(key, 11)
    shape = (SAMPLES, TEXT, HEADS * HEAD_DIM)
    base = jnp.clip(jax.random.normal(key, shape, jnp.float32), -5.0, 5.0)
    return base.astype(jnp.bfloat16)


def draw_image_keys(key, part):
    key = jax.random.fold_in(key, 12)
    shape = (KV_HEADS * 2, SLOTS, HALF, HEAD_DIM)
    base = jnp.clip(jax.random.normal(key, shape, jnp.float32), -5.0, 5.0)
    return base.astype(jnp.bfloat16)


def draw_image_counts(key, part):
    key = jax.random.fold_in(key, 13)
    key_counts, key_spots = jax.random.split(key, 2)
    counts = jax.random.randint(key_counts, (SAMPLES,), 1, MAX_TILES + 1)
    spots = jax.random.permutation(key_spots, SAMPLES)
    index = jnp.arange(SAMPLES)
    counts = jnp.where(index == spots[0], MAX_TILES, counts)
    counts = jnp.where(index == spots[1], 1, counts)
    return counts.astype(jnp.int32)


def draw_text_lengths(key, part):
    key = jax.random.fold_in(key, 14)
    key_lengths, key_spots = jax.random.split(key, 2)
    lengths = jax.random.randint(key_lengths, (SAMPLES,), TEXT // 4, TEXT + 1)
    spots = jax.random.permutation(key_spots, SAMPLES)
    index = jnp.arange(SAMPLES)
    lengths = jnp.where(index == spots[0], TEXT, lengths)
    lengths = jnp.where(index == spots[1], TEXT // 4, lengths)
    return lengths.astype(jnp.int32)


def draw_tile_owner(key, part):
    key = jax.random.fold_in(key, 15)
    groups = SAMPLES // SAMP_DEV
    row_keys = jax.random.split(key, groups)
    owners = jax.vmap(lambda row_key: jax.random.permutation(row_key, SAMP_DEV * MAX_TILES))(row_keys)
    return owners.reshape(SAMPLES, MAX_TILES).astype(jnp.int32)


def levels(stream_key, dims, cuts, least, top_value):
    gain, own = 1.0, jax.random.fold_in(stream_key, 6)
    for position, parts in cuts:
        steps = jnp.exp(jax.random.uniform(jax.random.fold_in(own, position), (parts,), jnp.float32, least / len(cuts), top_value / len(cuts)))
        gain = gain * jnp.repeat(steps, dims[position] // parts).reshape([-1 if axis == position else 1 for axis in range(len(dims))])
    return gain


def bell_draw(stream_key, extent, width, reach, shards=(), held_as=jnp.bfloat16):
    factor_of = levels(stream_key, extent, shards, -0.22, 0.18) if shards else 1.0
    entries = jax.random.normal(stream_key, extent, jnp.float32) * width * factor_of
    return jnp.minimum(jnp.maximum(entries, -reach), reach).astype(held_as)


def setup_inputs(seed: int = 0) -> dict:
    key_of = jax.random.split(jax.random.key(seed), 9)
    queries = draw_queries(jax.random.fold_in(key_of[8], 71), 0)
    grad_output = bell_draw(key_of[1], (SAMPLES, TEXT, HEADS * HEAD_DIM), 1.0, 5.0, ((0, 16), (2, 16)))
    image_keys = draw_image_keys(jax.random.fold_in(key_of[8], 71), 0)
    image_values = bell_draw(key_of[3], (KV_HEADS * 2, SLOTS, HALF, HEAD_DIM), 1.0, 5.0, ((0, 16), (1, 16)))
    attn_gate = jnp.clip(jax.random.uniform(key_of[4], (1,), jnp.float32, 0.3, 1.2), 0.3, 1.2)
    image_counts = draw_image_counts(jax.random.fold_in(key_of[8], 71), 0)
    text_lengths = draw_text_lengths(jax.random.fold_in(key_of[8], 71), 0)
    tile_owner = draw_tile_owner(jax.random.fold_in(key_of[8], 71), 0)
    return dict(queries=queries, grad_output=grad_output, image_keys=image_keys, image_values=image_values, attn_gate=attn_gate, image_counts=image_counts, text_lengths=text_lengths, tile_owner=tile_owner)


masked_score = -1.0e30


def to_tiles(stored):
    joined = stored.reshape(KV_HEADS, 2, SLOTS, HALF, HEAD_DIM)
    return jnp.transpose(joined, (0, 2, 1, 3, 4)).reshape(KV_HEADS, SLOTS, TILE, HEAD_DIM)


def from_tiles(tiles):
    split = tiles.reshape(KV_HEADS, SLOTS, 2, HALF, HEAD_DIM)
    return jnp.transpose(split, (0, 2, 1, 3, 4)).reshape(KV_HEADS * 2, SLOTS, HALF, HEAD_DIM)


def reference(queries, grad_output, image_keys, image_values, attn_gate, image_counts, text_lengths, tile_owner):
    score_scale = HEAD_DIM ** -0.5
    key_count = MAX_TILES * TILE
    gate_gain = jnp.tanh(attn_gate[0])
    row_live = (jnp.arange(TEXT)[None, :] < text_lengths[:, None]).astype(jnp.float32)
    grad_rows = (gate_gain * grad_output.astype(jnp.float32) * row_live[:, :, None]).astype(jnp.bfloat16)
    key_tiles = to_tiles(image_keys)
    value_tiles = to_tiles(image_values)
    device_index = (jnp.arange(SAMPLES) // SAMP_DEV).astype(jnp.int32)
    slot_index = (tile_owner * N_DP + device_index[:, None]).astype(jnp.int32)
    tile_live = jnp.arange(MAX_TILES)[None, :] < image_counts[:, None]
    key_live = jnp.repeat(tile_live, TILE, axis=1)

    def per_sample(sample_items):
        query, grad, slots, live = sample_items
        key_rows = key_tiles[:, slots].reshape(KV_HEADS, key_count, HEAD_DIM).astype(jnp.float32)
        value_rows = value_tiles[:, slots].reshape(KV_HEADS, key_count, HEAD_DIM).astype(jnp.float32)
        query_heads = query.astype(jnp.float32).reshape(TEXT, KV_HEADS, Q_GROUP, HEAD_DIM)
        grad_heads = grad.astype(jnp.float32).reshape(TEXT, KV_HEADS, Q_GROUP, HEAD_DIM)
        scores = jnp.einsum("tcgd,ckd->cgtk", query_heads, key_rows) * score_scale
        scores = jnp.where(live[None, None, None, :], scores, masked_score)
        row_top = jnp.max(scores, axis=-1, keepdims=True)
        exponent = jnp.exp(scores - row_top)
        weights = exponent / jnp.sum(exponent, axis=-1, keepdims=True)
        grad_weights = jnp.einsum("tcgd,ckd->cgtk", grad_heads, value_rows)
        row_delta = jnp.sum(weights * grad_weights, axis=-1, keepdims=True)
        grad_scores = (weights * (grad_weights - row_delta)).astype(jnp.bfloat16).astype(jnp.float32)
        weights_low = weights.astype(jnp.bfloat16).astype(jnp.float32)
        query_grad = (jnp.einsum("cgtk,ckd->tcgd", grad_scores, key_rows) * score_scale).astype(jnp.bfloat16)
        scores_sets = grad_scores.reshape(KV_HEADS, 2, HEADS_DEV, TEXT, key_count)
        weights_sets = weights_low.reshape(KV_HEADS, 2, HEADS_DEV, TEXT, key_count)
        query_sets = query_heads.reshape(TEXT, KV_HEADS, 2, HEADS_DEV, HEAD_DIM)
        grad_sets = grad_heads.reshape(TEXT, KV_HEADS, 2, HEADS_DEV, HEAD_DIM)
        key_part = (jnp.einsum("cshtk,tcshd->cskd", scores_sets, query_sets) * score_scale).astype(jnp.bfloat16)
        value_part = jnp.einsum("cshtk,tcshd->cskd", weights_sets, grad_sets).astype(jnp.bfloat16)
        key_grad = jnp.sum(key_part.astype(jnp.float32), axis=1).astype(jnp.bfloat16)
        value_grad = jnp.sum(value_part.astype(jnp.float32), axis=1).astype(jnp.bfloat16)
        return (query_grad.reshape(TEXT, HEADS * HEAD_DIM),
                key_grad.reshape(KV_HEADS, MAX_TILES, TILE, HEAD_DIM),
                value_grad.reshape(KV_HEADS, MAX_TILES, TILE, HEAD_DIM))

    grad_queries, key_all, value_all = lax.map(per_sample, (queries, grad_rows, slot_index, key_live))
    flat_slots = slot_index.reshape(-1)
    key_slots = jnp.transpose(key_all, (1, 0, 2, 3, 4)).reshape(KV_HEADS, SAMPLES * MAX_TILES, TILE, HEAD_DIM)
    value_slots = jnp.transpose(value_all, (1, 0, 2, 3, 4)).reshape(KV_HEADS, SAMPLES * MAX_TILES, TILE, HEAD_DIM)
    key_out = jnp.zeros((KV_HEADS, SLOTS, TILE, HEAD_DIM), jnp.bfloat16).at[:, flat_slots].set(key_slots)
    value_out = jnp.zeros((KV_HEADS, SLOTS, TILE, HEAD_DIM), jnp.bfloat16).at[:, flat_slots].set(value_slots)
    return grad_queries, from_tiles(key_out), from_tiles(value_out)
```

```python
import functools
import math

import jax
import jax.numpy as jnp
from jax import lax
from jax.experimental import pallas as pl
from jax.experimental.pallas import tpu as pltpu
from jax.sharding import PartitionSpec as P

MESH = pl.DeviceIdType.MESH
F32 = jnp.float32
BF16 = jnp.bfloat16
NT = (((1,), (1,)), ((), ()))
NN = (((1,), (0,)), ((), ()))
dead_offset = 1e37


def dot(a, b, dims=NN):
    return lax.dot_general(a, b, dims, preferred_element_type=F32)


def swap_sets(rows):
    half = rows.shape[0] // 2
    return jnp.concatenate((rows[half:], rows[:half]), 0)


def kernel(
    n_dp,
    counts,
    lengths,
    owners,
    gate,
    q_hbm,
    g_hbm,
    k_hbm,
    v_hbm,
    dq_out,
    dk_out,
    dv_out,
    slot_tile,
    qbuf,
    graw,
    gt,
    kbuf,
    vbuf,
    kt,
    vt,
    pbuf,
    sbuf,
    stat_own,
    stat_got,
    cbuf,
    d_own,
    d_got,
    dbuf,
    dvs,
    dks,
    dq_give,
    dq_own,
    dq_got,
    dq_stage,
    k_send,
    k_recv,
    v_send,
    v_recv,
    dv_send,
    dv_recv,
    dk_send,
    dk_recv,
    q_send,
    q_recv,
    g_send,
    g_recv,
    st_send,
    st_recv,
    d_send,
    d_recv,
    dq_send,
    dq_recv,
    local,
    out_sem,
):
    samples, text, _ = q_hbm.shape
    half_tile, head_dim = kbuf.shape[1:]
    heads = q_hbm.shape[2] // head_dim
    both = 2 * heads
    tiles = owners.shape[1]
    set_rows = heads * text
    scale = head_dim ** (-0.5)
    to_log2 = scale * math.log2(math.e)

    me = lax.axis_index("dp")
    side = lax.axis_index("tensor")
    mate = side + 1 - 2 * (side % 2)

    def peer(i):
        return (me + (2 * (i % 2) - 1) * ((i + 1) // 2) + n_dp) % n_dp

    def to_dp(src, dst, send, recv, other):
        return pltpu.make_async_remote_copy(
            src, dst, send, recv, device_id={"dp": other}, device_id_type=MESH
        )

    def to_mate(src, dst, send, recv):
        return pltpu.make_async_remote_copy(
            src, dst, send, recv, device_id={"tensor": mate}, device_id_type=MESH
        )

    def k_copy(other):
        return to_dp(k_hbm.at[other], kbuf.at[me], k_send.at[other], k_recv.at[me], other)

    def v_copy(other):
        return to_dp(v_hbm.at[other], vbuf.at[me], v_send.at[other], v_recv.at[me], other)

    def dv_copy(other):
        return to_dp(dvs.at[other], dv_out.at[me], dv_send.at[other], dv_recv.at[me], other)

    def dk_copy(other):
        return to_dp(dks.at[other], dk_out.at[me], dk_send.at[other], dk_recv.at[me], other)

    def landed(buf, recv, other):
        to_dp(buf.at[other], buf.at[other], recv.at[other], recv.at[other], other).wait_recv()

    def head_cols(ref, h):
        return ref.at[:, :, pl.ds(h * head_dim, head_dim)]

    def head_rows(ref, hh):
        return ref.at[:, pl.ds(hh * text, text), :]

    def q_copy(h):
        return to_mate(
            head_cols(q_hbm, h), head_rows(qbuf, heads + h), q_send.at[h], q_recv.at[h]
        )

    def g_copy(h):
        return to_mate(
            head_cols(g_hbm, h), head_rows(graw, heads + h), g_send.at[h], g_recv.at[h]
        )

    def stat_copy(b):
        return to_mate(stat_own.at[b], stat_got.at[b], st_send.at[b], st_recv.at[b])

    def d_copy(b):
        return to_mate(d_own.at[b], d_got.at[b], d_send.at[b], d_recv.at[b])

    def dq_copy(b):
        return to_mate(dq_give.at[b], dq_got.at[b], dq_send.at[b], dq_recv.at[b])

    barrier = pltpu.get_barrier_semaphore()

    def greet(i, _):
        pl.semaphore_signal(
            barrier, inc=1, device_id={"dp": peer(i)}, device_id_type=MESH
        )
        return 0

    lax.fori_loop(1, n_dp, greet, 0)
    pl.semaphore_signal(barrier, inc=1, device_id={"tensor": mate}, device_id_type=MESH)
    pl.semaphore_wait(barrier, n_dp)

    def start_k(i, _):
        k_copy(peer(i)).start()
        return 0

    lax.fori_loop(1, n_dp, start_k, 0)
    for h in range(heads):
        q_copy(h).start()
    here = [
        pltpu.make_async_copy(k_hbm.at[me], kbuf.at[me], local.at[0]),
        pltpu.make_async_copy(v_hbm.at[me], vbuf.at[me], local.at[1]),
    ]
    for h in range(heads):
        here.append(
            pltpu.make_async_copy(head_cols(q_hbm, h), head_rows(qbuf, h), local.at[2 + 2 * h])
        )
        here.append(
            pltpu.make_async_copy(head_cols(g_hbm, h), head_rows(graw, h), local.at[3 + 2 * h])
        )
    for copy in here:
        copy.start()

    def find_tile(o, _):
        tile = jnp.int32(0)
        for b in range(samples):
            for j in range(tiles):
                tile = jnp.where(owners[b, j] == o, b * tiles + j, tile)
        slot_tile[o] = tile
        return 0

    lax.fori_loop(0, n_dp, find_tile, 0)
    for copy in here:
        copy.wait()

    def next_v(i, _):
        k_copy(peer(i)).wait_send()
        v_copy(peer(i)).start()
        return 0

    step = (n_dp + heads - 1) // heads
    for h in range(heads):
        lax.fori_loop(max(1, h * step), min(n_dp, (h + 1) * step), next_v, 0)
        q_copy(h).wait_send()
        g_copy(h).start()

    def wait_k(i, _):
        landed(kbuf, k_recv, peer(i))
        return 0

    lax.fori_loop(1, n_dp, wait_k, 0)
    for h in range(heads):
        q_copy(h).wait_recv()

    chunk = 32

    def weigh(b):
        def one_head(hh, _):
            row = pl.multiple_of(hh * text, text)
            q = qbuf[b, pl.ds(row, text), :]
            count = counts[b]
            top = None
            for j in range(tiles):
                s = dot(kbuf[owners[b, j]], q, NT)
                sbuf[j] = s
                tile_top = jnp.max(s, axis=0, keepdims=True)
                top = (
                    tile_top
                    if top is None
                    else jnp.maximum(top, jnp.where(j < count, tile_top, -1e37))
                )
            top = top * to_log2
            total = jnp.zeros((8, text), F32)
            for j in range(tiles):
                off = jnp.where(j < count, top, dead_offset)
                for r in range(half_tile // chunk):
                    x = sbuf[j, r * chunk : (r + 1) * chunk, :]
                    p = jnp.exp2(x * to_log2 - off)
                    total = total + jnp.sum(p.reshape(chunk // 8, 8, text), axis=0)
                    pbuf[b * tiles + j, r * chunk : (r + 1) * chunk, pl.ds(row, text)] = (
                        p.astype(BF16)
                    )
            stat_own[b, 0, pl.ds(hh, 1), :] = top
            stat_own[b, 1, pl.ds(hh, 1), :] = jnp.sum(total, axis=0, keepdims=True)
            return 0

        lax.fori_loop(0, both, one_head, 0)

    def weigh_sample(b, _):
        weigh(b)
        stat_copy(b).start()
        return 0

    lax.fori_loop(0, samples, weigh_sample, 0)

    gain = jnp.tanh(jnp.full((1, text), gate[0], F32))

    def join_stats(b, _):
        stat_copy(b).wait()
        top, total = stat_own[b, 0], stat_own[b, 1]
        top_got, total_got = swap_sets(stat_got[b, 0]), swap_sets(stat_got[b, 1])
        peak = jnp.maximum(top, top_got)
        mine = jnp.exp2(top - peak)
        cbuf[b] = mine / (total * mine + total_got * jnp.exp2(top_got - peak))
        return 0

    lax.fori_loop(0, samples, join_stats, 0)

    def scale_grad(first):
        def one(it, _):
            b = it // heads
            hh = first + it % heads
            row = pl.multiple_of(hh * text, text)
            x = graw[b, pl.ds(row, text), :].astype(F32).T
            live = lax.broadcasted_iota(jnp.int32, x.shape, 1) < lengths[b]
            x = jnp.where(live, x * gain, 0.0).astype(BF16).astype(F32)
            gt[b, :, pl.ds(row, text)] = (x * cbuf[b, pl.ds(hh, 1), :]).astype(BF16)
            return 0

        lax.fori_loop(0, samples * heads, one, 0)

    scale_grad(0)
    for h in range(heads):
        g_copy(h).wait_recv()
    scale_grad(heads)

    def value_tile(o):
        tile = slot_tile[o]
        b = tile // tiles
        total = jnp.zeros((half_tile, head_dim), F32)
        for hh in range(both):
            cols = slice(hh * text, (hh + 1) * text)
            total = total + dot(pbuf[tile, :, cols], gt[b, :, cols], NT)
        dvs[o] = total.astype(BF16)

    def key_tile(o):
        tile = slot_tile[o]
        b = tile // tiles
        total = jnp.zeros((half_tile, head_dim), F32)
        for hh in range(both):
            cols = slice(hh * text, (hh + 1) * text)
            total = total + dot(pbuf[tile, :, cols], qbuf[b, cols, :])
        dks[o] = (total * scale).astype(BF16)

    def give_value(i, _):
        value_tile(peer(i))
        dv_copy(peer(i)).start()
        return 0

    lax.fori_loop(1, n_dp, give_value, 0)
    value_tile(me)
    dv_keep = pltpu.make_async_copy(dvs.at[me], dv_out.at[me], out_sem.at[0])
    dv_keep.start()

    def wait_v(i, _):
        landed(vbuf, v_recv, peer(i))
        return 0

    lax.fori_loop(1, n_dp, wait_v, 0)

    def turn(it, _):
        b, j = it // tiles, it % tiles
        own = owners[b, j]
        kt[it] = kbuf[own].astype(F32).T.astype(BF16)
        vt[it] = vbuf[own].astype(F32).T.astype(BF16)
        return 0

    lax.fori_loop(0, samples * tiles, turn, 0)

    def delta_sample(b, _):
        def one_head(hh, _):
            row = pl.multiple_of(hh * text, text)
            total = jnp.zeros((head_dim, text), F32)
            for j in range(tiles):
                total = total + dot(vt[b * tiles + j], pbuf[b * tiles + j, :, pl.ds(row, text)])
            d_own[b, pl.ds(hh, 1), :] = jnp.sum(
                total * gt[b, :, pl.ds(row, text)].astype(F32), axis=0, keepdims=True
            )
            return 0

        lax.fori_loop(0, both, one_head, 0)
        d_copy(b).start()
        return 0

    lax.fori_loop(0, samples, delta_sample, 0)

    def score_sample(b, _):
        d_copy(b).wait()
        dbuf[...] = cbuf[b] * (d_own[b] + swap_sets(d_got[b]))

        def one_head(hh):
            row = pl.multiple_of(hh * text, text)
            g = gt[b, :, pl.ds(row, text)]
            delta = dbuf[pl.ds(hh, 1), :]
            total = jnp.zeros((head_dim, text), F32)
            for j in range(tiles):
                at = b * tiles + j
                gw = dot(vbuf[owners[b, j]], g)
                ds = (pbuf[at, :, pl.ds(row, text)].astype(F32) * (gw - delta)).astype(BF16)
                pbuf[at, :, pl.ds(row, text)] = ds
                total = total + dot(kt[at], ds)
            return (total * scale).T

        def give_head(h, _):
            dq_give[b, h] = one_head(heads + h).astype(BF16)
            return 0

        def keep_head(h, _):
            dq_own[b, h] = one_head(h)
            return 0

        lax.fori_loop(0, heads, give_head, 0)
        dq_copy(b).start()
        lax.fori_loop(0, heads, keep_head, 0)
        return 0

    lax.fori_loop(0, samples, score_sample, 0)

    def give_key(i, _):
        key_tile(peer(i))
        dk_copy(peer(i)).start()
        return 0

    lax.fori_loop(1, n_dp, give_key, 0)
    key_tile(me)
    dk_keep = pltpu.make_async_copy(dks.at[me], dk_out.at[me], out_sem.at[1])
    dk_keep.start()

    def join_queries(b, _):
        dq_copy(b).wait()
        for h in range(heads):
            dq_stage[b, :, h * head_dim : (h + 1) * head_dim] = (
                dq_own[b, h] + dq_got[b, h].astype(F32)
            ).astype(BF16)
        return 0

    lax.fori_loop(0, samples, join_queries, 0)
    dq_keep = pltpu.make_async_copy(dq_stage, dq_out, out_sem.at[2])
    dq_keep.start()

    for h in range(heads):
        g_copy(h).wait_send()

    def finish(i, _):
        other = peer(i)
        v_copy(other).wait_send()
        dv_copy(other).wait_send()
        dk_copy(other).wait_send()
        landed(dv_out, dv_recv, other)
        landed(dk_out, dk_recv, other)
        return 0

    lax.fori_loop(1, n_dp, finish, 0)
    dv_keep.wait()
    dk_keep.wait()
    dq_keep.wait()


def shards(
    n_dp,
    queries,
    grad_output,
    image_keys,
    image_values,
    attn_gate,
    image_counts,
    text_lengths,
    tile_owner,
):
    samples, text, width = queries.shape
    _, slots, half_tile, head_dim = image_keys.shape
    heads = width // head_dim
    both = 2 * heads
    tiles = tile_owner.shape[1]
    rows = both * text
    stored = (slots, half_tile, head_dim)
    smem = pl.BlockSpec(memory_space=pltpu.SMEM)
    hbm = pl.BlockSpec(memory_space=pl.ANY)
    dma = pltpu.SemaphoreType.DMA
    dq, dk, dv = pl.pallas_call(
        functools.partial(kernel, n_dp),
        out_shape=(
            jax.ShapeDtypeStruct(queries.shape, BF16),
            jax.ShapeDtypeStruct(stored, BF16),
            jax.ShapeDtypeStruct(stored, BF16),
        ),
        in_specs=[smem] * 4 + [hbm] * 4,
        out_specs=(hbm, hbm, hbm),
        scratch_shapes=[
            pltpu.SMEM((slots,), jnp.int32),
            pltpu.VMEM((samples, rows, head_dim), BF16),
            pltpu.VMEM((samples, rows, head_dim), BF16),
            pltpu.VMEM((samples, head_dim, rows), BF16),
            pltpu.VMEM(stored, BF16),
            pltpu.VMEM(stored, BF16),
            pltpu.VMEM((slots, head_dim, half_tile), BF16),
            pltpu.VMEM((slots, head_dim, half_tile), BF16),
            pltpu.VMEM((slots, half_tile, rows), BF16),
            pltpu.VMEM((tiles, half_tile, text), F32),
            pltpu.VMEM((samples, 2, both, text), F32),
            pltpu.VMEM((samples, 2, both, text), F32),
            pltpu.VMEM((samples, both, text), F32),
            pltpu.VMEM((samples, both, text), F32),
            pltpu.VMEM((samples, both, text), F32),
            pltpu.VMEM((both, text), F32),
            pltpu.VMEM(stored, BF16),
            pltpu.VMEM(stored, BF16),
            pltpu.VMEM((samples, heads, text, head_dim), BF16),
            pltpu.VMEM((samples, heads, text, head_dim), F32),
            pltpu.VMEM((samples, heads, text, head_dim), BF16),
            pltpu.VMEM((samples, text, width), BF16),
        ]
        + [dma((slots,))] * 8
        + [dma((heads,))] * 4
        + [dma((samples,))] * 6
        + [dma((2 + 2 * heads,)), dma((3,))],
        compiler_params=pltpu.CompilerParams(
            collective_id=0, has_side_effects=True, vmem_limit_bytes=56 * 2**20
        ),
        name="cross_attention_backward",
    )(
        image_counts,
        text_lengths,
        tile_owner,
        attn_gate,
        queries,
        grad_output,
        image_keys[0],
        image_values[0],
    )
    return dq, dk[None], dv[None]


def solution(mesh):
    return jax.shard_map(
        functools.partial(shards, mesh.shape["dp"]),
        mesh=mesh,
        in_specs=(
            P("dp", None, "tensor"),
            P("dp", None, "tensor"),
            P("tensor", "dp", None, None),
            P("tensor", "dp", None, None),
            P(),
            P("dp"),
            P("dp"),
            P("dp", None),
        ),
        out_specs=(
            P("dp", None, "tensor"),
            P("tensor", "dp", None, None),
            P("tensor", "dp", None, None),
        ),
        check_vma=False,
    )
```

```python
import functools
import math

import jax
import jax.numpy as jnp
from jax import lax
from jax.experimental import pallas as pl
from jax.experimental.pallas import tpu as pltpu
from jax.sharding import PartitionSpec as P

MESH = pl.DeviceIdType.MESH
F32 = jnp.float32
BF16 = jnp.bfloat16
NT = (((1,), (1,)), ((), ()))
NN = (((1,), (0,)), ((), ()))
dead_offset = 1e37
group_size = 2


def dot(a, b, dims=NN):
    return lax.dot_general(a, b, dims, preferred_element_type=F32)


def swap_sets(rows):
    half = rows.shape[0] // 2
    return jnp.concatenate((rows[half:], rows[:half]), 0)


def kernel(
    n_dp,
    counts,
    lengths,
    owners,
    gate,
    q_hbm,
    g_hbm,
    k_hbm,
    v_hbm,
    dq_out,
    dk_out,
    dv_out,
    slot_tile,
    qbuf,
    graw,
    gt,
    kbuf,
    vbuf,
    kt,
    vt,
    pbuf,
    sbuf,
    stat_own,
    stat_got,
    cbuf,
    d_own,
    d_got,
    dbuf,
    dv_part,
    dvs,
    dks,
    dq_give,
    dq_own,
    dq_got,
    dq_stage,
    k_send,
    k_recv,
    v_send,
    v_recv,
    dv_send,
    dv_recv,
    dk_send,
    dk_recv,
    q_send,
    q_recv,
    g_send,
    g_recv,
    st_send,
    st_recv,
    d_send,
    d_recv,
    dq_send,
    dq_recv,
    local,
    out_sem,
):
    samples, text, _ = q_hbm.shape
    half_tile, head_dim = kbuf.shape[1:]
    heads = q_hbm.shape[2] // head_dim
    both = 2 * heads
    tiles = owners.shape[1]
    set_rows = heads * text
    scale = head_dim ** (-0.5)
    to_log2 = scale * math.log2(math.e)

    me = lax.axis_index("dp")
    side = lax.axis_index("tensor")
    mate = side + 1 - 2 * (side % 2)

    def peer(i):
        near = n_dp - i
        return (me + (2 * (near % 2) - 1) * ((near + 1) // 2) + n_dp) % n_dp

    def to_dp(src, dst, send, recv, other):
        return pltpu.make_async_remote_copy(
            src, dst, send, recv, device_id={"dp": other}, device_id_type=MESH
        )

    def to_mate(src, dst, send, recv):
        return pltpu.make_async_remote_copy(
            src, dst, send, recv, device_id={"tensor": mate}, device_id_type=MESH
        )

    def k_copy(other):
        return to_dp(k_hbm.at[other], kbuf.at[me], k_send.at[other], k_recv.at[me], other)

    def v_copy(other):
        return to_dp(v_hbm.at[other], vbuf.at[me], v_send.at[other], v_recv.at[me], other)

    def dv_copy(other):
        return to_dp(dvs.at[other], dv_out.at[me], dv_send.at[other], dv_recv.at[me], other)

    def dk_copy(other):
        return to_dp(dks.at[other], dk_out.at[me], dk_send.at[other], dk_recv.at[me], other)

    def landed(buf, recv, other):
        to_dp(buf.at[other], buf.at[other], recv.at[other], recv.at[other], other).wait_recv()

    def q_copy(b):
        return to_mate(q_hbm.at[b], qbuf.at[1, b], q_send.at[b], q_recv.at[b])

    def g_copy(b):
        return to_mate(g_hbm.at[b], graw.at[1, b], g_send.at[b], g_recv.at[b])

    def stat_copy(b):
        return to_mate(stat_own.at[b], stat_got.at[b], st_send.at[b], st_recv.at[b])

    def d_copy(b):
        return to_mate(d_own.at[b], d_got.at[b], d_send.at[b], d_recv.at[b])

    def dq_copy(b):
        return to_mate(dq_give.at[b], dq_got.at[b], dq_send.at[b], dq_recv.at[b])

    barrier = pltpu.get_barrier_semaphore()

    def greet(i, _):
        pl.semaphore_signal(
            barrier, inc=1, device_id={"dp": peer(i)}, device_id_type=MESH
        )
        return 0

    lax.fori_loop(1, n_dp, greet, 0)
    pl.semaphore_signal(barrier, inc=1, device_id={"tensor": mate}, device_id_type=MESH)
    pl.semaphore_wait(barrier, n_dp)

    def start_k(i, _):
        k_copy(peer(i)).start()
        return 0

    lax.fori_loop(1, n_dp, start_k, 0)
    for b in range(samples):
        q_copy(b).start()
    here = [
        pltpu.make_async_copy(k_hbm.at[me], kbuf.at[me], local.at[0]),
        pltpu.make_async_copy(v_hbm.at[me], vbuf.at[me], local.at[1]),
        pltpu.make_async_copy(q_hbm, qbuf.at[0], local.at[2]),
        pltpu.make_async_copy(g_hbm, graw.at[0], local.at[3]),
    ]
    for copy in here:
        copy.start()

    def find_tile(o, _):
        tile = jnp.int32(0)
        for b in range(samples):
            for j in range(tiles):
                tile = jnp.where(owners[b, j] == o, b * tiles + j, tile)
        slot_tile[o] = tile
        return 0

    lax.fori_loop(0, n_dp, find_tile, 0)
    for copy in here:
        copy.wait()

    def sent_k(i, _):
        k_copy(peer(i)).wait_send()
        return 0

    def start_v(i, _):
        v_copy(peer(i)).start()
        return 0

    for b in range(samples):
        q_copy(b).wait_send()
        g_copy(b).start()
    lax.fori_loop(1, n_dp, sent_k, 0)
    lax.fori_loop(1, n_dp, start_v, 0)

    def wait_k(i, _):
        landed(kbuf, k_recv, peer(i))
        return 0

    lax.fori_loop(1, n_dp, wait_k, 0)
    for b in range(samples):
        q_copy(b).wait_recv()

    chunk = 32

    def cols_of(h):
        return slice(h * head_dim, (h + 1) * head_dim)

    def rows_of(hh):
        return slice(hh * text, (hh + 1) * text)

    def weigh(b):
        def one_set(which, _):
            count = counts[b]
            for h in range(heads):
                hh = which * heads + h
                row = pl.multiple_of(hh * text, text)
                q = qbuf[which, b, :, cols_of(h)]
                top = None
                for j in range(tiles):
                    s = dot(kbuf[owners[b, j]], q, NT)
                    sbuf[h, j] = s
                    tile_top = jnp.max(s, axis=0, keepdims=True)
                    top = (
                        tile_top
                        if top is None
                        else jnp.maximum(top, jnp.where(j < count, tile_top, -1e37))
                    )
                top = top * to_log2
                total = jnp.zeros((8, text), F32)
                for j in range(tiles):
                    off = jnp.where(j < count, top, dead_offset)
                    for r in range(half_tile // chunk):
                        x = sbuf[h, j, r * chunk : (r + 1) * chunk, :]
                        p = jnp.exp2(x * to_log2 - off)
                        total = total + jnp.sum(p.reshape(chunk // 8, 8, text), axis=0)
                        pbuf[b * tiles + j, r * chunk : (r + 1) * chunk, pl.ds(row, text)] = (
                            p.astype(BF16)
                        )
                stat_own[b, 0, pl.ds(hh, 1), :] = top
                stat_own[b, 1, pl.ds(hh, 1), :] = jnp.sum(total, axis=0, keepdims=True)
            return 0

        lax.fori_loop(0, 2, one_set, 0)

    def weigh_sample(b, _):
        weigh(b)
        stat_copy(b).start()
        return 0

    lax.fori_loop(0, samples, weigh_sample, 0)

    gain = jnp.tanh(jnp.full((1, text), gate[0], F32))

    def join_stats(b, _):
        stat_copy(b).wait()
        top, total = stat_own[b, 0], stat_own[b, 1]
        top_got, total_got = swap_sets(stat_got[b, 0]), swap_sets(stat_got[b, 1])
        peak = jnp.maximum(top, top_got)
        mine = jnp.exp2(top - peak)
        cbuf[b] = mine / (total * mine + total_got * jnp.exp2(top_got - peak))
        return 0

    lax.fori_loop(0, samples, join_stats, 0)

    def scale_grad(which, b):
        live = lax.broadcasted_iota(jnp.int32, (head_dim, text), 1) < lengths[b]
        for h in range(heads):
            hh = which * heads + h
            x = graw[which, b, :, cols_of(h)].astype(F32).T
            x = jnp.where(live, x * gain, 0.0).astype(BF16).astype(F32)
            gt[b, :, rows_of(hh)] = (x * cbuf[b, hh : hh + 1, :]).astype(BF16)

    def value_sum(o, first):
        tile = slot_tile[o]
        b = tile // tiles
        total = jnp.zeros((half_tile, head_dim), F32)
        for hh in range(first, first + heads):
            total = total + dot(pbuf[tile, :, rows_of(hh)], gt[b, :, rows_of(hh)], NT)
        return total

    def scale_own(b, _):
        scale_grad(0, b)
        return 0

    lax.fori_loop(0, samples, scale_own, 0)

    def start_value(o, _):
        dv_part[o] = value_sum(o, 0)
        return 0

    lax.fori_loop(0, n_dp, start_value, 0, unroll=4)

    def turn_keys(it, _):
        kt[it] = kbuf[owners[it // tiles, it % tiles]].astype(F32).T.astype(BF16)
        return 0

    lax.fori_loop(0, samples * tiles, turn_keys, 0, unroll=4)
    def scale_got(b, _):
        g_copy(b).wait_recv()
        scale_grad(1, b)
        return 0

    lax.fori_loop(0, samples, scale_got, 0)

    def value_tile(o):
        dvs[o] = (dv_part[o] + value_sum(o, heads)).astype(BF16)

    def key_tile(o):
        tile = slot_tile[o]
        b = tile // tiles
        total = jnp.zeros((half_tile, head_dim), F32)
        for hh in range(both):
            total = total + dot(
                pbuf[tile, :, rows_of(hh)], qbuf[hh // heads, b, :, cols_of(hh % heads)]
            )
        dks[o] = (total * scale).astype(BF16)

    def give_values(i, _):
        group = [peer(group_size * i + 2 + k) for k in range(group_size)]
        for other in group:
            value_tile(other)
        for other in group:
            dv_copy(other).start()
        return 0

    value_tile(peer(1))
    dv_copy(peer(1)).start()
    lax.fori_loop(0, (n_dp - 2) // group_size, give_values, 0)
    value_tile(me)
    dv_keep = pltpu.make_async_copy(dvs.at[me], dv_out.at[me], out_sem.at[0])
    dv_keep.start()

    def wait_v(i, _):
        landed(vbuf, v_recv, peer(i))
        return 0

    lax.fori_loop(1, n_dp, wait_v, 0)

    def turn_values(it, _):
        vt[it] = vbuf[owners[it // tiles, it % tiles]].astype(F32).T.astype(BF16)
        return 0

    lax.fori_loop(0, samples * tiles, turn_values, 0, unroll=4)

    def delta_sample(b, _):
        def one_head(hh, _):
            row = pl.multiple_of(hh * text, text)
            total = jnp.zeros((head_dim, text), F32)
            for j in range(tiles):
                total = total + dot(vt[b * tiles + j], pbuf[b * tiles + j, :, pl.ds(row, text)])
            d_own[b, pl.ds(hh, 1), :] = jnp.sum(
                total * gt[b, :, pl.ds(row, text)].astype(F32), axis=0, keepdims=True
            )
            return 0

        lax.fori_loop(0, both, one_head, 0, unroll=4)
        d_copy(b).start()
        return 0

    lax.fori_loop(0, samples, delta_sample, 0)

    def score_sample(b, _):
        d_copy(b).wait()
        dbuf[...] = cbuf[b] * (d_own[b] + swap_sets(d_got[b]))

        def one_head(hh):
            row = pl.multiple_of(hh * text, text)
            g = gt[b, :, pl.ds(row, text)]
            delta = dbuf[pl.ds(hh, 1), :]
            total = jnp.zeros((head_dim, text), F32)
            for j in range(tiles):
                at = b * tiles + j
                gw = dot(vbuf[owners[b, j]], g)
                ds = (pbuf[at, :, pl.ds(row, text)].astype(F32) * (gw - delta)).astype(BF16)
                pbuf[at, :, pl.ds(row, text)] = ds
                total = total + dot(kt[at], ds)
            return (total * scale).T

        def give_head(h, _):
            dq_give[b, h] = one_head(heads + h).astype(BF16)
            return 0

        def keep_head(h, _):
            dq_own[b, h] = one_head(h)
            return 0

        lax.fori_loop(0, heads, give_head, 0, unroll=4)
        dq_copy(b).start()
        lax.fori_loop(0, heads, keep_head, 0, unroll=4)
        return 0

    lax.fori_loop(0, samples, score_sample, 0)

    def give_keys(i, _):
        group = [peer(group_size * i + 2 + k) for k in range(group_size)]
        for other in group:
            key_tile(other)
        for other in group:
            dk_copy(other).start()
        return 0

    key_tile(peer(1))
    dk_copy(peer(1)).start()
    lax.fori_loop(0, (n_dp - 2) // group_size, give_keys, 0)
    key_tile(me)
    dk_keep = pltpu.make_async_copy(dks.at[me], dk_out.at[me], out_sem.at[1])
    dk_keep.start()

    def join_queries(b, _):
        dq_copy(b).wait()
        for h in range(heads):
            dq_stage[b, :, h * head_dim : (h + 1) * head_dim] = (
                dq_own[b, h] + dq_got[b, h].astype(F32)
            ).astype(BF16)
        return 0

    lax.fori_loop(0, samples, join_queries, 0)
    dq_keep = pltpu.make_async_copy(dq_stage, dq_out, out_sem.at[2])
    dq_keep.start()

    for b in range(samples):
        g_copy(b).wait_send()

    def finish(i, _):
        other = peer(i)
        v_copy(other).wait_send()
        dv_copy(other).wait_send()
        dk_copy(other).wait_send()
        landed(dv_out, dv_recv, other)
        landed(dk_out, dk_recv, other)
        return 0

    lax.fori_loop(1, n_dp, finish, 0)
    dv_keep.wait()
    dk_keep.wait()
    dq_keep.wait()


def place(dq, dk, dv, dq_out, dk_out, dv_out, dq_buf, dk_buf, dv_buf, get_sem, put_sem):
    moves = []
    for src, buf, dst in ((dq, dq_buf, dq_out), (dk, dk_buf, dk_out), (dv, dv_buf, dv_out)):
        half = src.shape[0] // 2
        for part in (pl.ds(0, half), pl.ds(half, half)):
            at = len(moves)
            moves.append(
                (
                    pltpu.make_async_copy(src.at[part], buf.at[part], get_sem.at[at]),
                    pltpu.make_async_copy(buf.at[part], dst.at[part], put_sem.at[at]),
                )
            )
    for get, _ in moves:
        get.start()
    for get, put in moves:
        get.wait()
        put.start()
    for _, put in moves:
        put.wait()


def shards(
    n_dp,
    queries,
    grad_output,
    image_keys,
    image_values,
    attn_gate,
    image_counts,
    text_lengths,
    tile_owner,
):
    samples, text, width = queries.shape
    _, slots, half_tile, head_dim = image_keys.shape
    heads = width // head_dim
    both = 2 * heads
    tiles = tile_owner.shape[1]
    rows = both * text
    stored = (slots, half_tile, head_dim)
    smem = pl.BlockSpec(memory_space=pltpu.SMEM)
    hbm = pl.BlockSpec(memory_space=pl.ANY)
    dma = pltpu.SemaphoreType.DMA
    results = (
        jax.ShapeDtypeStruct(queries.shape, BF16),
        jax.ShapeDtypeStruct(stored, BF16),
        jax.ShapeDtypeStruct(stored, BF16),
    )
    made = pl.pallas_call(
        functools.partial(kernel, n_dp),
        out_shape=results,
        in_specs=[smem] * 4 + [hbm] * 4,
        out_specs=(hbm, hbm, hbm),
        scratch_shapes=[
            pltpu.SMEM((slots,), jnp.int32),
            pltpu.VMEM((2,) + queries.shape, BF16),
            pltpu.VMEM((2,) + queries.shape, BF16),
            pltpu.VMEM((samples, head_dim, rows), BF16),
            pltpu.VMEM(stored, BF16),
            pltpu.VMEM(stored, BF16),
            pltpu.VMEM((slots, head_dim, half_tile), BF16),
            pltpu.VMEM((slots, head_dim, half_tile), BF16),
            pltpu.VMEM((slots, half_tile, rows), BF16),
            pltpu.VMEM((heads, tiles, half_tile, text), F32),
            pltpu.VMEM((samples, 2, both, text), F32),
            pltpu.VMEM((samples, 2, both, text), F32),
            pltpu.VMEM((samples, both, text), F32),
            pltpu.VMEM((samples, both, text), F32),
            pltpu.VMEM((samples, both, text), F32),
            pltpu.VMEM((both, text), F32),
            pltpu.VMEM(stored, F32),
            pltpu.VMEM(stored, BF16),
            pltpu.VMEM(stored, BF16),
            pltpu.VMEM((samples, heads, text, head_dim), BF16),
            pltpu.VMEM((samples, heads, text, head_dim), F32),
            pltpu.VMEM((samples, heads, text, head_dim), BF16),
            pltpu.VMEM((samples, text, width), BF16),
        ]
        + [dma((slots,))] * 8
        + [dma((samples,))] * 10
        + [dma((4,)), dma((3,))],
        compiler_params=pltpu.CompilerParams(
            collective_id=0, has_side_effects=True, vmem_limit_bytes=56 * 2**20
        ),
        name="cross_attention_backward",
    )(
        image_counts,
        text_lengths,
        tile_owner,
        attn_gate,
        queries,
        grad_output,
        image_keys[0],
        image_values[0],
    )
    dq, dk, dv = pl.pallas_call(
        place,
        out_shape=results,
        in_specs=[hbm] * 3,
        out_specs=(hbm, hbm, hbm),
        scratch_shapes=[pltpu.VMEM(leaf.shape, BF16) for leaf in results] + [dma((6,))] * 2,
        name="place_results",
    )(*made)
    return dq, dk[None], dv[None]


def solution(mesh):
    return jax.shard_map(
        functools.partial(shards, mesh.shape["dp"]),
        mesh=mesh,
        in_specs=(
            P("dp", None, "tensor"),
            P("dp", None, "tensor"),
            P("tensor", "dp", None, None),
            P("tensor", "dp", None, None),
            P(),
            P("dp"),
            P("dp"),
            P("dp", None),
        ),
        out_specs=(
            P("dp", None, "tensor"),
            P("tensor", "dp", None, None),
            P("tensor", "dp", None, None),
        ),
        check_vma=False,
    )
```

```python
import functools
import math

import jax
import jax.numpy as jnp
from jax import lax
from jax.experimental import pallas as pl
from jax.experimental.pallas import tpu as pltpu
from jax.sharding import PartitionSpec as P

MESH = pl.DeviceIdType.MESH
F32 = jnp.float32
BF16 = jnp.bfloat16
NT = (((1,), (1,)), ((), ()))
NN = (((1,), (0,)), ((), ()))
dead_offset = 1e37
value_group = 2
group_size = 2


def dot(a, b, dims=NN):
    return lax.dot_general(a, b, dims, preferred_element_type=F32)


def swap_sets(rows):
    half = rows.shape[0] // 2
    return jnp.concatenate((rows[half:], rows[:half]), 0)


def kernel(
    n_dp,
    counts,
    lengths,
    owners,
    gate,
    q_hbm,
    g_hbm,
    k_hbm,
    v_hbm,
    dq_out,
    dk_out,
    dv_out,
    slot_tile,
    qbuf,
    graw,
    gt,
    kbuf,
    vbuf,
    kt,
    vt,
    pbuf,
    sbuf,
    stat_own,
    stat_got,
    cbuf,
    d_own,
    d_got,
    dbuf,
    dv_part,
    dvs,
    dks,
    dq_give,
    dq_own,
    dq_got,
    dq_stage,
    k_send,
    k_recv,
    v_send,
    v_recv,
    dv_send,
    dv_recv,
    dk_send,
    dk_recv,
    q_send,
    q_recv,
    g_send,
    g_recv,
    st_send,
    st_recv,
    d_send,
    d_recv,
    dq_send,
    dq_recv,
    q_local,
    g_local,
    tile_local,
    out_sem,
):
    samples, text, _ = q_hbm.shape
    half_tile, head_dim = kbuf.shape[1:]
    heads = q_hbm.shape[2] // head_dim
    both = 2 * heads
    tiles = owners.shape[1]
    early = heads // 2
    scale = head_dim ** (-0.5)
    to_log2 = scale * math.log2(math.e)

    me = lax.axis_index("dp")
    side = lax.axis_index("tensor")
    mate = side + 1 - 2 * (side % 2)

    def peer(i):
        near = n_dp - i
        return (me + (2 * (near % 2) - 1) * ((near + 1) // 2) + n_dp) % n_dp

    def to_dp(src, dst, send, recv, other):
        return pltpu.make_async_remote_copy(
            src, dst, send, recv, device_id={"dp": other}, device_id_type=MESH
        )

    def to_mate(src, dst, send, recv):
        return pltpu.make_async_remote_copy(
            src, dst, send, recv, device_id={"tensor": mate}, device_id_type=MESH
        )

    def k_copy(other):
        return to_dp(k_hbm.at[other], kbuf.at[me], k_send.at[other], k_recv.at[me], other)

    def v_copy(other):
        return to_dp(v_hbm.at[other], vbuf.at[me], v_send.at[other], v_recv.at[me], other)

    def dv_copy(other):
        return to_dp(dvs.at[other], dv_out.at[me], dv_send.at[other], dv_recv.at[me], other)

    def dk_copy(other):
        return to_dp(dks.at[other], dk_out.at[me], dk_send.at[other], dk_recv.at[me], other)

    def landed(buf, recv, other):
        to_dp(buf.at[other], buf.at[other], recv.at[other], recv.at[other], other).wait_recv()

    def q_copy(b):
        return to_mate(q_hbm.at[b], qbuf.at[1, b], q_send.at[b], q_recv.at[b])

    def g_copy(h):
        return to_mate(graw.at[0, h], graw.at[1, h], g_send.at[h], g_recv.at[h])

    def stat_copy(b):
        return to_mate(stat_own.at[b], stat_got.at[b], st_send.at[b], st_recv.at[b])

    def d_copy(b):
        return to_mate(d_own.at[b], d_got.at[b], d_send.at[b], d_recv.at[b])

    def dq_copy(b):
        return to_mate(dq_give.at[b], dq_got.at[b], dq_send.at[b], dq_recv.at[b])

    q_here = [
        pltpu.make_async_copy(q_hbm.at[b], qbuf.at[0, b], q_local.at[b]) for b in range(samples)
    ]
    g_here = [
        pltpu.make_async_copy(
            g_hbm.at[:, :, pl.ds(h * head_dim, head_dim)], graw.at[0, h], g_local.at[h]
        )
        for h in range(heads)
    ]
    tile_here = [
        pltpu.make_async_copy(k_hbm.at[me], kbuf.at[me], tile_local.at[0]),
        pltpu.make_async_copy(v_hbm.at[me], vbuf.at[me], tile_local.at[1]),
    ]
    barrier = pltpu.get_barrier_semaphore()

    def greet(i, _):
        pl.semaphore_signal(
            barrier, inc=1, device_id={"dp": peer(i)}, device_id_type=MESH
        )
        return 0

    lax.fori_loop(1, n_dp, greet, 0, unroll=True)
    pl.semaphore_signal(barrier, inc=1, device_id={"tensor": mate}, device_id_type=MESH)
    pl.semaphore_wait(barrier, n_dp)

    def start_k(i, _):
        k_copy(peer(i)).start()
        return 0

    lax.fori_loop(1, n_dp, start_k, 0, unroll=True)
    for b in range(samples):
        q_copy(b).start()
    for copy in q_here + g_here + tile_here:
        copy.start()

    def find_tile(o, _):
        tile = jnp.int32(0)
        for b in range(samples):
            for j in range(tiles):
                tile = jnp.where(owners[b, j] == o, b * tiles + j, tile)
        slot_tile[o] = tile
        return 0

    lax.fori_loop(0, n_dp, find_tile, 0)
    for copy in q_here + g_here + tile_here:
        copy.wait()

    def sent_k(i, _):
        k_copy(peer(i)).wait_send()
        return 0

    def start_v(i, _):
        v_copy(peer(i)).start()
        return 0

    for b in range(samples):
        q_copy(b).wait_send()
    for h in range(early):
        g_copy(h).start()
    lax.fori_loop(1, n_dp, sent_k, 0)
    lax.fori_loop(1, n_dp, start_v, 0, unroll=True)

    def wait_k(i, _):
        landed(kbuf, k_recv, peer(i))
        return 0

    lax.fori_loop(1, n_dp, wait_k, 0)
    for b in range(samples):
        q_copy(b).wait_recv()

    chunk = 32

    def cols_of(h):
        return slice(h * head_dim, (h + 1) * head_dim)

    def rows_of(hh):
        return slice(hh * text, (hh + 1) * text)

    def weigh(b):
        def one_set(which, _):
            count = counts[b]
            for h in range(heads):
                hh = which * heads + h
                row = pl.multiple_of(hh * text, text)
                q = qbuf[which, b, :, cols_of(h)]
                top = None
                for j in range(tiles):
                    s = dot(kbuf[owners[b, j]], q, NT)
                    sbuf[h, j] = s
                    tile_top = jnp.max(s, axis=0, keepdims=True)
                    top = (
                        tile_top
                        if top is None
                        else jnp.maximum(top, jnp.where(j < count, tile_top, -1e37))
                    )
                top = top * to_log2
                total = jnp.zeros((8, text), F32)
                for j in range(tiles):
                    off = jnp.where(j < count, top, dead_offset)
                    for r in range(half_tile // chunk):
                        x = sbuf[h, j, r * chunk : (r + 1) * chunk, :]
                        p = jnp.exp2(x * to_log2 - off)
                        total = total + jnp.sum(p.reshape(chunk // 8, 8, text), axis=0)
                        pbuf[b * tiles + j, r * chunk : (r + 1) * chunk, pl.ds(row, text)] = (
                            p.astype(BF16)
                        )
                stat_own[b, 0, pl.ds(hh, 1), :] = top
                stat_own[b, 1, pl.ds(hh, 1), :] = jnp.sum(total, axis=0, keepdims=True)
            return 0

        lax.fori_loop(0, 2, one_set, 0)

    def weigh_sample(b, _):
        weigh(b)
        stat_copy(b).start()
        return 0

    lax.fori_loop(0, samples // 2, weigh_sample, 0)
    for h in range(early):
        g_copy(h).wait_send()
    for h in range(early, heads):
        g_copy(h).start()
    lax.fori_loop(samples // 2, samples, weigh_sample, 0)

    gain = jnp.tanh(jnp.full((1, text), gate[0], F32))

    def join_stats(b, _):
        stat_copy(b).wait()
        top, total = stat_own[b, 0], stat_own[b, 1]
        top_got, total_got = swap_sets(stat_got[b, 0]), swap_sets(stat_got[b, 1])
        peak = jnp.maximum(top, top_got)
        mine = jnp.exp2(top - peak)
        cbuf[b] = mine / (total * mine + total_got * jnp.exp2(top_got - peak))
        return 0

    lax.fori_loop(0, samples, join_stats, 0)

    def scale_grad(which, h):
        rows = rows_of(which * heads + h)

        def one(b, _):
            x = graw[which, h, b].astype(F32).T
            live = lax.broadcasted_iota(jnp.int32, x.shape, 1) < lengths[b]
            x = jnp.where(live, x * gain, 0.0).astype(BF16).astype(F32)
            factor = cbuf[b, which * heads + h : which * heads + h + 1, :]
            gt[b, :, rows] = (x * factor).astype(BF16)
            return 0

        lax.fori_loop(0, samples, one, 0, unroll=4)

    def value_sum(o, first, number):
        tile = slot_tile[o]
        b = tile // tiles
        total = jnp.zeros((half_tile, head_dim), F32)
        for hh in range(first, first + number):
            total = total + dot(pbuf[tile, :, rows_of(hh)], gt[b, :, rows_of(hh)], NT)
        return total

    for h in range(heads):
        scale_grad(0, h)
    for h in range(early):
        g_copy(h).wait_recv()
        scale_grad(1, h)

    def start_value(o, _):
        dv_part[o] = value_sum(o, 0, heads + early)
        return 0

    lax.fori_loop(0, n_dp, start_value, 0, unroll=4)
    for h in range(early, heads):
        g_copy(h).wait_recv()
        scale_grad(1, h)

    def value_tile(o):
        dvs[o] = (dv_part[o] + value_sum(o, heads + early, heads - early)).astype(BF16)

    def key_tile(o):
        tile = slot_tile[o]
        b = tile // tiles
        total = jnp.zeros((half_tile, head_dim), F32)
        for hh in range(both):
            total = total + dot(
                pbuf[tile, :, rows_of(hh)], qbuf[hh // heads, b, :, cols_of(hh % heads)]
            )
        dks[o] = (total * scale).astype(BF16)

    def give_values(i, _):
        group = [peer(value_group * i + 2 + k) for k in range(value_group)]
        for other in group:
            value_tile(other)
        for other in group:
            dv_copy(other).start()
        return 0

    value_tile(peer(1))
    dv_copy(peer(1)).start()
    lax.fori_loop(0, (n_dp - 2) // value_group, give_values, 0)
    value_tile(me)
    dv_keep = pltpu.make_async_copy(dvs.at[me], dv_out.at[me], out_sem.at[0])
    dv_keep.start()

    def turn_keys(it, _):
        kt[it] = kbuf[owners[it // tiles, it % tiles]].astype(F32).T.astype(BF16)
        return 0

    lax.fori_loop(0, samples * tiles, turn_keys, 0, unroll=4)

    def wait_v(i, _):
        landed(vbuf, v_recv, peer(i))
        return 0

    lax.fori_loop(1, n_dp, wait_v, 0)

    def turn_values(it, _):
        vt[it] = vbuf[owners[it // tiles, it % tiles]].astype(F32).T.astype(BF16)
        return 0

    lax.fori_loop(0, samples * tiles, turn_values, 0, unroll=4)

    def delta_sample(b, _):
        def one_head(hh, _):
            row = pl.multiple_of(hh * text, text)
            total = jnp.zeros((head_dim, text), F32)
            for j in range(tiles):
                total = total + dot(vt[b * tiles + j], pbuf[b * tiles + j, :, pl.ds(row, text)])
            d_own[b, pl.ds(hh, 1), :] = jnp.sum(
                total * gt[b, :, pl.ds(row, text)].astype(F32), axis=0, keepdims=True
            )
            return 0

        lax.fori_loop(0, both, one_head, 0, unroll=4)
        d_copy(b).start()
        return 0

    lax.fori_loop(0, samples, delta_sample, 0)

    def score_sample(b, _):
        d_copy(b).wait()
        dbuf[...] = cbuf[b] * (d_own[b] + swap_sets(d_got[b]))

        def one_head(hh):
            row = pl.multiple_of(hh * text, text)
            g = gt[b, :, pl.ds(row, text)]
            delta = dbuf[pl.ds(hh, 1), :]
            total = jnp.zeros((head_dim, text), F32)
            for j in range(tiles):
                at = b * tiles + j
                gw = dot(vbuf[owners[b, j]], g)
                ds = (pbuf[at, :, pl.ds(row, text)].astype(F32) * (gw - delta)).astype(BF16)
                pbuf[at, :, pl.ds(row, text)] = ds
                total = total + dot(kt[at], ds)
            return (total * scale).T

        def give_head(h, _):
            dq_give[b, h] = one_head(heads + h).astype(BF16)
            return 0

        def keep_head(h, _):
            dq_own[b, h] = one_head(h)
            return 0

        lax.fori_loop(0, heads, give_head, 0, unroll=4)
        dq_copy(b).start()
        lax.fori_loop(0, heads, keep_head, 0, unroll=4)
        return 0

    lax.fori_loop(0, samples, score_sample, 0)

    def give_keys(i, _):
        group = [peer(group_size * i + 2 + k) for k in range(group_size)]
        for other in group:
            key_tile(other)
        for other in group:
            dk_copy(other).start()
        return 0

    key_tile(peer(1))
    dk_copy(peer(1)).start()
    lax.fori_loop(0, (n_dp - 2) // group_size, give_keys, 0)
    key_tile(me)
    dk_keep = pltpu.make_async_copy(dks.at[me], dk_out.at[me], out_sem.at[1])
    dk_keep.start()

    def join_queries(b, _):
        dq_copy(b).wait()
        for h in range(heads):
            dq_stage[b, :, h * head_dim : (h + 1) * head_dim] = (
                dq_own[b, h] + dq_got[b, h].astype(F32)
            ).astype(BF16)
        return 0

    lax.fori_loop(0, samples, join_queries, 0)
    dq_keep = pltpu.make_async_copy(dq_stage, dq_out, out_sem.at[2])
    dq_keep.start()

    for h in range(early, heads):
        g_copy(h).wait_send()

    def finish_values(i, _):
        other = peer(i)
        v_copy(other).wait_send()
        dv_copy(other).wait_send()
        landed(dv_out, dv_recv, other)
        return 0

    def finish_sent(i, _):
        dk_copy(peer(i)).wait_send()
        return 0

    def finish_keys(i, _):
        landed(dk_out, dk_recv, peer(i))
        return 0

    lax.fori_loop(1, n_dp, finish_values, 0)
    lax.fori_loop(1, n_dp, finish_sent, 0)
    lax.fori_loop(1, n_dp, finish_keys, 0)
    dv_keep.wait()
    dk_keep.wait()
    dq_keep.wait()


def place(dq, dk, dv, dq_out, dk_out, dv_out, dq_buf, dk_buf, dv_buf, get_sem, put_sem):
    moves = []
    for src, buf, dst in ((dq, dq_buf, dq_out), (dk, dk_buf, dk_out), (dv, dv_buf, dv_out)):
        half = src.shape[0] // 2
        for part in (pl.ds(0, half), pl.ds(half, half)):
            at = len(moves)
            moves.append(
                (
                    pltpu.make_async_copy(src.at[part], buf.at[part], get_sem.at[at]),
                    pltpu.make_async_copy(buf.at[part], dst.at[part], put_sem.at[at]),
                )
            )
    for get, _ in moves:
        get.start()
    for get, put in moves:
        get.wait()
        put.start()
    for _, put in moves:
        put.wait()


def shards(
    n_dp,
    queries,
    grad_output,
    image_keys,
    image_values,
    attn_gate,
    image_counts,
    text_lengths,
    tile_owner,
):
    samples, text, width = queries.shape
    _, slots, half_tile, head_dim = image_keys.shape
    heads = width // head_dim
    both = 2 * heads
    tiles = tile_owner.shape[1]
    rows = both * text
    stored = (slots, half_tile, head_dim)
    smem = pl.BlockSpec(memory_space=pltpu.SMEM)
    hbm = pl.BlockSpec(memory_space=pl.ANY)
    dma = pltpu.SemaphoreType.DMA
    results = (
        jax.ShapeDtypeStruct(queries.shape, BF16),
        jax.ShapeDtypeStruct(stored, BF16),
        jax.ShapeDtypeStruct(stored, BF16),
    )
    made = pl.pallas_call(
        functools.partial(kernel, n_dp),
        out_shape=results,
        in_specs=[smem] * 4 + [hbm] * 4,
        out_specs=(hbm, hbm, hbm),
        scratch_shapes=[
            pltpu.SMEM((slots,), jnp.int32),
            pltpu.VMEM((2,) + queries.shape, BF16),
            pltpu.VMEM((2, heads, samples, text, head_dim), BF16),
            pltpu.VMEM((samples, head_dim, rows), BF16),
            pltpu.VMEM(stored, BF16),
            pltpu.VMEM(stored, BF16),
            pltpu.VMEM((slots, head_dim, half_tile), BF16),
            pltpu.VMEM((slots, head_dim, half_tile), BF16),
            pltpu.VMEM((slots, half_tile, rows), BF16),
            pltpu.VMEM((heads, tiles, half_tile, text), F32),
            pltpu.VMEM((samples, 2, both, text), F32),
            pltpu.VMEM((samples, 2, both, text), F32),
            pltpu.VMEM((samples, both, text), F32),
            pltpu.VMEM((samples, both, text), F32),
            pltpu.VMEM((samples, both, text), F32),
            pltpu.VMEM((both, text), F32),
            pltpu.VMEM(stored, F32),
            pltpu.VMEM(stored, BF16),
            pltpu.VMEM(stored, BF16),
            pltpu.VMEM((samples, heads, text, head_dim), BF16),
            pltpu.VMEM((samples, heads, text, head_dim), F32),
            pltpu.VMEM((samples, heads, text, head_dim), BF16),
            pltpu.VMEM((samples, text, width), BF16),
        ]
        + [dma((slots,))] * 8
        + [dma((samples,))] * 2
        + [dma((heads,))] * 2
        + [dma((samples,))] * 6
        + [dma((samples,)), dma((heads,)), dma((2,)), dma((3,))],
        compiler_params=pltpu.CompilerParams(
            collective_id=0, has_side_effects=True, vmem_limit_bytes=56 * 2**20
        ),
        name="cross_attention_backward",
    )(
        image_counts,
        text_lengths,
        tile_owner,
        attn_gate,
        queries,
        grad_output,
        image_keys[0],
        image_values[0],
    )
    dq, dk, dv = pl.pallas_call(
        place,
        out_shape=results,
        in_specs=[hbm] * 3,
        out_specs=(hbm, hbm, hbm),
        scratch_shapes=[pltpu.VMEM(leaf.shape, BF16) for leaf in results] + [dma((6,))] * 2,
        name="place_results",
    )(*made)
    return dq, dk[None], dv[None]


def solution(mesh):
    return jax.shard_map(
        functools.partial(shards, mesh.shape["dp"]),
        mesh=mesh,
        in_specs=(
            P("dp", None, "tensor"),
            P("dp", None, "tensor"),
            P("tensor", "dp", None, None),
            P("tensor", "dp", None, None),
            P(),
            P("dp"),
            P("dp"),
            P("dp", None),
        ),
        out_specs=(
            P("dp", None, "tensor"),
            P("tensor", "dp", None, None),
            P("tensor", "dp", None, None),
        ),
        check_vma=False,
    )
```

```python
import functools
import math

import jax
import jax.numpy as jnp
from jax import lax
from jax.experimental import pallas as pl
from jax.experimental.pallas import tpu as pltpu
from jax.sharding import PartitionSpec as P

MESH = pl.DeviceIdType.MESH
F32 = jnp.float32
BF16 = jnp.bfloat16
NT = (((1,), (1,)), ((), ()))
NN = (((1,), (0,)), ((), ()))
dead_offset = 1e37
group_size = 2


def dot(a, b, dims=NN):
    return lax.dot_general(a, b, dims, preferred_element_type=F32)


def swap_sets(rows):
    half = rows.shape[0] // 2
    return jnp.concatenate((rows[half:], rows[:half]), 0)


def kernel(
    n_dp,
    counts,
    lengths,
    owners,
    gate,
    q_hbm,
    g_hbm,
    k_hbm,
    v_hbm,
    dq_out,
    dk_out,
    dv_out,
    slot_tile,
    qbuf,
    graw,
    gt,
    kbuf,
    vbuf,
    kt,
    vt,
    pbuf,
    sbuf,
    stat_own,
    stat_got,
    cbuf,
    d_own,
    d_got,
    dbuf,
    dv_part,
    dvs,
    dks,
    dq_give,
    dq_own,
    dq_got,
    dq_stage,
    k_send,
    k_recv,
    v_send,
    v_recv,
    dv_send,
    dv_recv,
    dk_send,
    dk_recv,
    q_send,
    q_recv,
    g_send,
    g_recv,
    st_send,
    st_recv,
    d_send,
    d_recv,
    dq_send,
    dq_recv,
    local,
    out_sem,
):
    samples, text, _ = q_hbm.shape
    half_tile, head_dim = kbuf.shape[1:]
    heads = q_hbm.shape[2] // head_dim
    both = 2 * heads
    tiles = owners.shape[1]
    set_rows = heads * text
    scale = head_dim ** (-0.5)
    to_log2 = scale * math.log2(math.e)

    me = lax.axis_index("dp")
    side = lax.axis_index("tensor")
    mate = side + 1 - 2 * (side % 2)

    def peer(i):
        near = n_dp - i
        return (me + (2 * (near % 2) - 1) * ((near + 1) // 2) + n_dp) % n_dp

    def to_dp(src, dst, send, recv, other):
        return pltpu.make_async_remote_copy(
            src, dst, send, recv, device_id={"dp": other}, device_id_type=MESH
        )

    def to_mate(src, dst, send, recv):
        return pltpu.make_async_remote_copy(
            src, dst, send, recv, device_id={"tensor": mate}, device_id_type=MESH
        )

    def k_copy(other):
        return to_dp(k_hbm.at[other], kbuf.at[me], k_send.at[other], k_recv.at[me], other)

    def v_copy(other):
        return to_dp(v_hbm.at[other], vbuf.at[me], v_send.at[other], v_recv.at[me], other)

    def dv_copy(other):
        return to_dp(dvs.at[other], dv_out.at[me], dv_send.at[other], dv_recv.at[me], other)

    def dk_copy(other):
        return to_dp(dks.at[other], dk_out.at[me], dk_send.at[other], dk_recv.at[me], other)

    def landed(buf, recv, other):
        to_dp(buf.at[other], buf.at[other], recv.at[other], recv.at[other], other).wait_recv()

    def q_copy(b):
        return to_mate(q_hbm.at[b], qbuf.at[1, b], q_send.at[b], q_recv.at[b])

    def g_copy(b):
        return to_mate(g_hbm.at[b], graw.at[1, b], g_send.at[b], g_recv.at[b])

    def stat_copy(b):
        return to_mate(stat_own.at[b], stat_got.at[b], st_send.at[b], st_recv.at[b])

    def d_copy(b):
        return to_mate(d_own.at[b], d_got.at[b], d_send.at[b], d_recv.at[b])

    def dq_copy(b):
        return to_mate(dq_give.at[b], dq_got.at[b], dq_send.at[b], dq_recv.at[b])

    barrier = pltpu.get_barrier_semaphore()

    def greet(i, _):
        pl.semaphore_signal(
            barrier, inc=1, device_id={"dp": peer(i)}, device_id_type=MESH
        )
        return 0

    lax.fori_loop(1, n_dp, greet, 0)
    pl.semaphore_signal(barrier, inc=1, device_id={"tensor": mate}, device_id_type=MESH)
    pl.semaphore_wait(barrier, n_dp)

    def start_k(i, _):
        k_copy(peer(i)).start()
        return 0

    lax.fori_loop(1, n_dp, start_k, 0)
    for b in range(samples):
        q_copy(b).start()
    here = [
        pltpu.make_async_copy(k_hbm.at[me], kbuf.at[me], local.at[0]),
        pltpu.make_async_copy(v_hbm.at[me], vbuf.at[me], local.at[1]),
        pltpu.make_async_copy(q_hbm, qbuf.at[0], local.at[2]),
        pltpu.make_async_copy(g_hbm, graw.at[0], local.at[3]),
    ]
    for copy in here:
        copy.start()

    def find_tile(o, _):
        tile = jnp.int32(0)
        for b in range(samples):
            for j in range(tiles):
                tile = jnp.where(owners[b, j] == o, b * tiles + j, tile)
        slot_tile[o] = tile
        return 0

    lax.fori_loop(0, n_dp, find_tile, 0)
    for copy in here:
        copy.wait()

    def sent_k(i, _):
        k_copy(peer(i)).wait_send()
        return 0

    def start_v(i, _):
        v_copy(peer(i)).start()
        return 0

    for b in range(samples):
        q_copy(b).wait_send()
        g_copy(b).start()
    lax.fori_loop(1, n_dp, sent_k, 0)
    lax.fori_loop(1, n_dp, start_v, 0)

    def wait_k(i, _):
        landed(kbuf, k_recv, peer(i))
        return 0

    lax.fori_loop(1, n_dp, wait_k, 0)
    for b in range(samples):
        q_copy(b).wait_recv()

    chunk = 32

    def cols_of(h):
        return slice(h * head_dim, (h + 1) * head_dim)

    def rows_of(hh):
        return slice(hh * text, (hh + 1) * text)

    def weigh(b):
        def one_set(which, _):
            count = counts[b]
            for h in range(heads):
                hh = which * heads + h
                row = pl.multiple_of(hh * text, text)
                q = qbuf[which, b, :, cols_of(h)]
                top = None
                for j in range(tiles):
                    s = dot(kbuf[owners[b, j]], q, NT)
                    sbuf[h, j] = s
                    tile_top = jnp.max(s, axis=0, keepdims=True)
                    top = (
                        tile_top
                        if top is None
                        else jnp.maximum(top, jnp.where(j < count, tile_top, -1e37))
                    )
                top = top * to_log2
                total = jnp.zeros((8, text), F32)
                for j in range(tiles):
                    off = jnp.where(j < count, top, dead_offset)
                    for r in range(half_tile // chunk):
                        x = sbuf[h, j, r * chunk : (r + 1) * chunk, :]
                        p = jnp.exp2(x * to_log2 - off)
                        total = total + jnp.sum(p.reshape(chunk // 8, 8, text), axis=0)
                        pbuf[b * tiles + j, r * chunk : (r + 1) * chunk, pl.ds(row, text)] = (
                            p.astype(BF16)
                        )
                stat_own[b, 0, pl.ds(hh, 1), :] = top
                stat_own[b, 1, pl.ds(hh, 1), :] = jnp.sum(total, axis=0, keepdims=True)
            return 0

        lax.fori_loop(0, 2, one_set, 0)

    def weigh_sample(b, _):
        weigh(b)
        stat_copy(b).start()
        return 0

    lax.fori_loop(0, samples, weigh_sample, 0)

    gain = jnp.tanh(jnp.full((1, text), gate[0], F32))

    def join_stats(b, _):
        stat_copy(b).wait()
        top, total = stat_own[b, 0], stat_own[b, 1]
        top_got, total_got = swap_sets(stat_got[b, 0]), swap_sets(stat_got[b, 1])
        peak = jnp.maximum(top, top_got)
        mine = jnp.exp2(top - peak)
        cbuf[b] = mine / (total * mine + total_got * jnp.exp2(top_got - peak))
        return 0

    lax.fori_loop(0, samples, join_stats, 0)

    def scale_grad(which, b):
        live = lax.broadcasted_iota(jnp.int32, (head_dim, text), 1) < lengths[b]
        for h in range(heads):
            hh = which * heads + h
            x = graw[which, b, :, cols_of(h)].astype(F32).T
            x = jnp.where(live, x * gain, 0.0).astype(BF16).astype(F32)
            gt[b, :, rows_of(hh)] = (x * cbuf[b, hh : hh + 1, :]).astype(BF16)

    def value_sum(o, first):
        tile = slot_tile[o]
        b = tile // tiles
        total = jnp.zeros((half_tile, head_dim), F32)
        for hh in range(first, first + heads):
            total = total + dot(pbuf[tile, :, rows_of(hh)], gt[b, :, rows_of(hh)], NT)
        return total

    def scale_own(b, _):
        scale_grad(0, b)
        return 0

    lax.fori_loop(0, samples, scale_own, 0)

    def start_value(o, _):
        dv_part[o] = value_sum(o, 0)
        return 0

    lax.fori_loop(0, n_dp, start_value, 0, unroll=4)

    def scale_got(b, _):
        g_copy(b).wait_recv()
        scale_grad(1, b)
        return 0

    lax.fori_loop(0, samples, scale_got, 0)

    def value_tile(o):
        dvs[o] = (dv_part[o] + value_sum(o, heads)).astype(BF16)

    def key_tile(o):
        tile = slot_tile[o]
        b = tile // tiles
        total = jnp.zeros((half_tile, head_dim), F32)
        for hh in range(both):
            total = total + dot(
                pbuf[tile, :, rows_of(hh)], qbuf[hh // heads, b, :, cols_of(hh % heads)]
            )
        dks[o] = (total * scale).astype(BF16)

    def give_values(i, _):
        group = [peer(group_size * i + 2 + k) for k in range(group_size)]
        for other in group:
            value_tile(other)
        for other in group:
            dv_copy(other).start()
        return 0

    value_tile(peer(1))
    dv_copy(peer(1)).start()
    lax.fori_loop(0, (n_dp - 2) // group_size, give_values, 0)
    value_tile(me)
    dv_keep = pltpu.make_async_copy(dvs.at[me], dv_out.at[me], out_sem.at[0])
    dv_keep.start()

    def turn_keys(it, _):
        kt[it] = kbuf[owners[it // tiles, it % tiles]].astype(F32).T.astype(BF16)
        return 0

    lax.fori_loop(0, samples * tiles, turn_keys, 0, unroll=4)

    def wait_v(i, _):
        landed(vbuf, v_recv, peer(i))
        return 0

    lax.fori_loop(1, n_dp, wait_v, 0)

    def turn_values(it, _):
        vt[it] = vbuf[owners[it // tiles, it % tiles]].astype(F32).T.astype(BF16)
        return 0

    lax.fori_loop(0, samples * tiles, turn_values, 0, unroll=4)

    def delta_sample(b, _):
        def one_head(hh, _):
            row = pl.multiple_of(hh * text, text)
            total = jnp.zeros((head_dim, text), F32)
            for j in range(tiles):
                total = total + dot(vt[b * tiles + j], pbuf[b * tiles + j, :, pl.ds(row, text)])
            d_own[b, pl.ds(hh, 1), :] = jnp.sum(
                total * gt[b, :, pl.ds(row, text)].astype(F32), axis=0, keepdims=True
            )
            return 0

        lax.fori_loop(0, both, one_head, 0, unroll=4)
        d_copy(b).start()
        return 0

    lax.fori_loop(0, samples, delta_sample, 0)

    def score_sample(b, _):
        d_copy(b).wait()
        dbuf[...] = cbuf[b] * (d_own[b] + swap_sets(d_got[b]))

        def one_head(hh):
            row = pl.multiple_of(hh * text, text)
            g = gt[b, :, pl.ds(row, text)]
            delta = dbuf[pl.ds(hh, 1), :]
            total = jnp.zeros((head_dim, text), F32)
            for j in range(tiles):
                at = b * tiles + j
                gw = dot(vbuf[owners[b, j]], g)
                ds = (pbuf[at, :, pl.ds(row, text)].astype(F32) * (gw - delta)).astype(BF16)
                pbuf[at, :, pl.ds(row, text)] = ds
                total = total + dot(kt[at], ds)
            return (total * scale).T

        def give_head(h, _):
            dq_give[b, h] = one_head(heads + h).astype(BF16)
            return 0

        def keep_head(h, _):
            dq_own[b, h] = one_head(h)
            return 0

        lax.fori_loop(0, heads, give_head, 0, unroll=4)
        dq_copy(b).start()
        lax.fori_loop(0, heads, keep_head, 0, unroll=4)
        return 0

    lax.fori_loop(0, samples, score_sample, 0)

    def give_keys(i, _):
        group = [peer(group_size * i + 2 + k) for k in range(group_size)]
        for other in group:
            key_tile(other)
        for other in group:
            dk_copy(other).start()
        return 0

    key_tile(peer(1))
    dk_copy(peer(1)).start()
    lax.fori_loop(0, (n_dp - 2) // group_size, give_keys, 0)
    key_tile(me)
    dk_keep = pltpu.make_async_copy(dks.at[me], dk_out.at[me], out_sem.at[1])
    dk_keep.start()

    def join_queries(b, _):
        dq_copy(b).wait()
        for h in range(heads):
            dq_stage[b, :, h * head_dim : (h + 1) * head_dim] = (
                dq_own[b, h] + dq_got[b, h].astype(F32)
            ).astype(BF16)
        return 0

    lax.fori_loop(0, samples, join_queries, 0)
    dq_keep = pltpu.make_async_copy(dq_stage, dq_out, out_sem.at[2])
    dq_keep.start()

    for b in range(samples):
        g_copy(b).wait_send()

    def finish(i, _):
        other = peer(i)
        v_copy(other).wait_send()
        dv_copy(other).wait_send()
        dk_copy(other).wait_send()
        landed(dv_out, dv_recv, other)
        landed(dk_out, dk_recv, other)
        return 0

    lax.fori_loop(1, n_dp, finish, 0)
    dv_keep.wait()
    dk_keep.wait()
    dq_keep.wait()


def place(dq, dk, dv, dq_out, dk_out, dv_out, dq_buf, dk_buf, dv_buf, get_sem, put_sem):
    moves = []
    for src, buf, dst in ((dq, dq_buf, dq_out), (dk, dk_buf, dk_out), (dv, dv_buf, dv_out)):
        half = src.shape[0] // 2
        for part in (pl.ds(0, half), pl.ds(half, half)):
            at = len(moves)
            moves.append(
                (
                    pltpu.make_async_copy(src.at[part], buf.at[part], get_sem.at[at]),
                    pltpu.make_async_copy(buf.at[part], dst.at[part], put_sem.at[at]),
                )
            )
    for get, _ in moves:
        get.start()
    for get, put in moves:
        get.wait()
        put.start()
    for _, put in moves:
        put.wait()


def shards(
    n_dp,
    queries,
    grad_output,
    image_keys,
    image_values,
    attn_gate,
    image_counts,
    text_lengths,
    tile_owner,
):
    samples, text, width = queries.shape
    _, slots, half_tile, head_dim = image_keys.shape
    heads = width // head_dim
    both = 2 * heads
    tiles = tile_owner.shape[1]
    rows = both * text
    stored = (slots, half_tile, head_dim)
    smem = pl.BlockSpec(memory_space=pltpu.SMEM)
    hbm = pl.BlockSpec(memory_space=pl.ANY)
    dma = pltpu.SemaphoreType.DMA
    results = (
        jax.ShapeDtypeStruct(queries.shape, BF16),
        jax.ShapeDtypeStruct(stored, BF16),
        jax.ShapeDtypeStruct(stored, BF16),
    )
    made = pl.pallas_call(
        functools.partial(kernel, n_dp),
        out_shape=results,
        in_specs=[smem] * 4 + [hbm] * 4,
        out_specs=(hbm, hbm, hbm),
        scratch_shapes=[
            pltpu.SMEM((slots,), jnp.int32),
            pltpu.VMEM((2,) + queries.shape, BF16),
            pltpu.VMEM((2,) + queries.shape, BF16),
            pltpu.VMEM((samples, head_dim, rows), BF16),
            pltpu.VMEM(stored, BF16),
            pltpu.VMEM(stored, BF16),
            pltpu.VMEM((slots, head_dim, half_tile), BF16),
            pltpu.VMEM((slots, head_dim, half_tile), BF16),
            pltpu.VMEM((slots, half_tile, rows), BF16),
            pltpu.VMEM((heads, tiles, half_tile, text), F32),
            pltpu.VMEM((samples, 2, both, text), F32),
            pltpu.VMEM((samples, 2, both, text), F32),
            pltpu.VMEM((samples, both, text), F32),
            pltpu.VMEM((samples, both, text), F32),
            pltpu.VMEM((samples, both, text), F32),
            pltpu.VMEM((both, text), F32),
            pltpu.VMEM(stored, F32),
            pltpu.VMEM(stored, BF16),
            pltpu.VMEM(stored, BF16),
            pltpu.VMEM((samples, heads, text, head_dim), BF16),
            pltpu.VMEM((samples, heads, text, head_dim), F32),
            pltpu.VMEM((samples, heads, text, head_dim), BF16),
            pltpu.VMEM((samples, text, width), BF16),
        ]
        + [dma((slots,))] * 8
        + [dma((samples,))] * 10
        + [dma((4,)), dma((3,))],
        compiler_params=pltpu.CompilerParams(
            collective_id=0, has_side_effects=True, vmem_limit_bytes=56 * 2**20
        ),
        name="cross_attention_backward",
    )(
        image_counts,
        text_lengths,
        tile_owner,
        attn_gate,
        queries,
        grad_output,
        image_keys[0],
        image_values[0],
    )
    dq, dk, dv = pl.pallas_call(
        place,
        out_shape=results,
        in_specs=[hbm] * 3,
        out_specs=(hbm, hbm, hbm),
        scratch_shapes=[pltpu.VMEM(leaf.shape, BF16) for leaf in results] + [dma((6,))] * 2,
        name="place_results",
    )(*made)
    return dq, dk[None], dv[None]


def solution(mesh):
    return jax.shard_map(
        functools.partial(shards, mesh.shape["dp"]),
        mesh=mesh,
        in_specs=(
            P("dp", None, "tensor"),
            P("dp", None, "tensor"),
            P("tensor", "dp", None, None),
            P("tensor", "dp", None, None),
            P(),
            P("dp"),
            P("dp"),
            P("dp", None),
        ),
        out_specs=(
            P("dp", None, "tensor"),
            P("tensor", "dp", None, None),
            P("tensor", "dp", None, None),
        ),
        check_vma=False,
    )
```
